256 devices in a mesh: row: 8 (over z_hi, core), col: 32 (over z_lo, y, x).
Axes of the slice: x: 4, y: 4, z: 8 (z_hi: 4, z_lo: 2; z = z_hi * 2 + z_lo), core: 2. Of those that a mesh axis runs over, the one named last changes fastest.
Arguments:
- tiles: bfloat16 [8, 32, 256, 128, 128], P('row', 'col'), may hold values from -0.046875 to 0.046875
- block_rows: int32 [8, 32, 256], P('row', 'col'), may hold values from 0 to 7
- block_cols: int32 [8, 32, 256], P('row', 'col'), may hold values from 0 to 31
- live: int32 [8, 32], P('row', 'col'), may hold values from 32 to 256, as said below
- seeds: float32 [32768, 64], P(('col', 'row')), may hold values from -6 to 6
- beta: float32 [64], replicated, may hold values from 0.3 to 0.9
Outputs:
- scores: float32 [32768, 64], P(('col', 'row'))
The draws below stay inside these ranges and needn't reach their ends.
Inputs may be any that keep to these rules, and one draw needn't show every extreme that they name: Some device has all 256 slots live and some device exactly 32; live counts differ strongly between devices.
All inputs are finite; a program needn't handle non-finite values.
Results may differ from the reference program's by a relative error of at most 0.0039.
Values may be sent and summed in bfloat16 or wider, within the bound.
A program may use at most 64 MiB of HBM per device.

```python
import math
import jax
import jax.numpy as jnp
import numpy as np
from jax import lax

BLK = 128
SEEDS = 64
PIECE = 128
SLOTS = 256
TERMS = 4
NODES = 32768
N_ROW = 8
N_COL = 32


def draw_live(key, part):
    key = jax.random.fold_in(key, 5)
    first, second = jax.random.split(key)
    lowest = SLOTS // 8
    spread = jax.random.randint(first, (N_ROW * N_COL,), 0, 65)
    counts = lowest + (SLOTS - lowest) * spread * spread // 4096
    order = jax.random.permutation(second, N_ROW * N_COL)
    counts = counts.at[order[0]].set(SLOTS).at[order[1]].set(lowest)
    return counts.reshape(N_ROW, N_COL).astype(jnp.int32)


def set_ends(result, rng, least, high):
    spot = [jax.random.randint(jax.random.fold_in(rng, axis), (), 0, length) for axis, length in enumerate(result.shape)]
    widest = result.shape.index(max(result.shape))
    next_to = spot[:widest] + [(spot[widest] + 1) % result.shape[widest]] + spot[widest + 1:]
    return result.at[tuple(spot)].set(least).at[tuple(next_to)].set(high)


def block_scale(own_key, shape, cuts, low, high):
    factor_of = 1.0
    for axis_at, blocks in cuts:
        draws = jax.random.uniform(jax.random.fold_in(jax.random.fold_in(own_key, 6), axis_at), (blocks,), jnp.float32, low / len(cuts), high / len(cuts))
        factor_of = factor_of * jnp.repeat(jnp.exp(draws), shape[axis_at] // blocks).reshape((-1,) + (1,) * (len(shape) - 1 - axis_at))
    return factor_of


def rank_table(amount, lean):
    portions = [(1 << 20) // math.isqrt(grade ** lean) + 1 for grade in range(1, amount + 1)]
    scale = 1 + sum(portions) // (1 << 30)
    return np.cumsum(np.array([max(1, weight // scale) for weight in portions]))


def skewed_ids(stream_key, dims, count, skew):
    listing = rank_table(count, skew)
    lot = jax.random.randint(jax.random.fold_in(stream_key, 1), dims, 0, int(listing[count - 1]))
    standing = jnp.searchsorted(jnp.asarray(listing, jnp.int32), lot, side="right")
    return jax.random.permutation(jax.random.fold_in(stream_key, 2), count)[standing].astype(jnp.int32)


def noise(own_key, shape, scale, limit, cuts=(), kind=jnp.bfloat16):
    array = jax.random.normal(own_key, shape, jnp.float32) * scale
    if len(cuts) > 0:
        array = block_scale(own_key, shape, cuts, -0.22, 0.18) * array
    return jnp.clip(array, min=-limit, max=limit).astype(kind)


def setup_inputs(seed: int = 0) -> dict:
    keys = jax.random.split(jax.random.key(seed), 7)
    return {
        "tiles": noise(keys[0], (N_ROW, N_COL, SLOTS, BLK, BLK), (BLK * SLOTS // 2) ** -0.5, 0.046875, ((0, 8), (1, 32))),
        "block_rows": set_ends(jax.random.randint(keys[1], (N_ROW, N_COL, SLOTS), 0, N_ROW * PIECE // BLK), jax.random.fold_in(keys[1], 1), 0, (N_ROW * PIECE // BLK) - 1).astype(jnp.int32),
        "block_cols": set_ends(skewed_ids(keys[2], (N_ROW, N_COL, SLOTS), N_COL * PIECE // BLK, 2), jax.random.fold_in(keys[2], 3), 0, (N_COL * PIECE // BLK) - 1).astype(jnp.int32),
        "live": draw_live(jax.random.fold_in(keys[6], 71), 0),
        "seeds": noise(keys[4], (NODES, SEEDS), 1.0, 6.0, ((0, 256),), jnp.float32),
        "beta": jnp.clip(jnp.exp(jax.random.uniform(keys[5], (SEEDS,), jnp.float32, math.log(0.3), math.log(0.9))), 0.3, 0.9),
    }


def reference(tiles, block_rows, block_cols, live, seeds, beta):
    row_blocks = N_ROW * PIECE // BLK
    col_blocks = N_COL * PIECE // BLK
    usable = (jnp.arange(SLOTS, dtype=jnp.int32)[None, None, :] < live[:, :, None]).astype(jnp.float32)
    scores = seeds
    for term in range(TERMS):
        current = lax.optimization_barrier(scores.astype(jnp.bfloat16)).astype(jnp.float32)
        grid = current.reshape(N_COL, N_ROW, PIECE, SEEDS)
        regions = grid.reshape(N_COL, row_blocks, BLK, SEEDS)

        def per_row(index):
            across = lax.dynamic_index_in_dim(grid, index, 1, False).reshape(col_blocks, BLK, SEEDS)
            tile = lax.dynamic_index_in_dim(tiles, index, 0, False).astype(jnp.float32)
            tile = tile * lax.dynamic_index_in_dim(usable, index, 0, False)[:, :, None, None]
            brow = lax.dynamic_index_in_dim(block_rows, index, 0, False)
            bcol = lax.dynamic_index_in_dim(block_cols, index, 0, False)
            incoming = across[bcol]
            fwd = jnp.einsum("csij,csjk->csik", tile, incoming)
            segment = (jnp.arange(N_COL, dtype=jnp.int32)[:, None] * row_blocks + brow).reshape(-1)
            forward = jax.ops.segment_sum(fwd.reshape(-1, BLK, SEEDS), segment, N_COL * row_blocks)
            downward = regions[jnp.arange(N_COL, dtype=jnp.int32)[:, None], brow]
            bwd = jnp.einsum("csji,csjk->csik", tile, downward)
            backward = jax.ops.segment_sum(bwd.reshape(-1, BLK, SEEDS), bcol.reshape(-1), col_blocks)
            return forward, backward

        forwards, backwards = lax.map(per_row, jnp.arange(N_ROW, dtype=jnp.int32))
        forward = jnp.sum(forwards, axis=0).reshape(N_COL, N_ROW, PIECE, SEEDS)
        backward = backwards.reshape(N_ROW, N_COL, PIECE, SEEDS).transpose(1, 0, 2, 3)
        total = (forward + backward).reshape(-1, SEEDS)
        scores = beta[None, :] * total + seeds
    return scores
```

```python
import functools

import jax
import jax.numpy as jnp
from jax import lax
from jax.experimental import pallas as pl
from jax.experimental.pallas import tpu as pltpu
from jax.sharding import PartitionSpec as P

TERMS = 4
MESH = pl.DeviceIdType.MESH
F32 = jnp.float32
BF16 = jnp.bfloat16
LAST = (((1,), (1,)), ((), ()))

XZ, XROW, XOWN, XOTHER, POTHER, POWN, PROW, PZ = range(8)


def kernel(
    side,
    idx,
    tiles,
    seeds,
    beta,
    out,
    raw,
    run,
    dense,
    xs,
    ys,
    bstage,
    fstage,
    bland,
    fland,
    zstage,
    zland,
    facc,
    seeds_t,
    beta_t,
    score,
    tile_sem,
    send_sem,
    recv_sem,
):
    slots = raw.shape[0]
    blk = raw.shape[1]
    n_row = ys.shape[1]
    n_col = xs.shape[1]
    plane = side * side
    parts = tile_sem.shape[0]
    chunk = slots // parts
    r = lax.axis_index("row")
    c = lax.axis_index("col")
    z = c // plane
    yx = c % plane
    y = yx // side
    x = yx % side
    partner = ((z + 1) % 2) * plane + yx

    def plane_peer(off):
        return ((y + off // side) % side) * side + (x + off % side) % side

    def row_peer(off):
        return (r + off) % n_row

    def tile_copy(i):
        part = pl.ds(i * chunk, chunk)
        return pltpu.make_async_copy(tiles.at[part], raw.at[part], tile_sem.at[i])

    for i in range(parts):
        tile_copy(i).start()

    def send(src, dst, t, kind, device):
        pltpu.make_async_remote_copy(
            src_ref=src,
            dst_ref=dst,
            send_sem=send_sem.at[t, kind],
            recv_sem=recv_sem.at[t, kind],
            device_id=device,
            device_id_type=MESH,
        ).start()

    def await_bytes(ref, sem):
        pltpu.make_async_copy(ref, ref, sem).wait()

    barrier = pltpu.get_barrier_semaphore()
    pl.semaphore_signal(barrier, inc=1, device_id=(r, partner), device_id_type=MESH)

    @pl.loop(1, plane)
    def _(off):
        pl.semaphore_signal(
            barrier, inc=1, device_id=(r, z * plane + plane_peer(off)), device_id_type=MESH
        )

    @pl.loop(1, n_row)
    def _(off):
        pl.semaphore_signal(barrier, inc=1, device_id=(row_peer(off), c), device_id_type=MESH)

    seeds_t[...] = seeds[...].T
    beta_t[...] = jnp.broadcast_to(beta[...], (blk, beta.shape[1])).T
    score[...] = seeds_t[...]
    pl.semaphore_wait(barrier, 1 + (plane - 1) + (n_row - 1))

    def spread(t):
        current = score[...].astype(BF16)
        xs[t, c] = current
        ys[t, r] = current
        send(xs.at[t, c], xs.at[t, c], t, XZ, (r, partner))

        @pl.loop(1, n_row)
        def _(off):
            send(ys.at[t, r], ys.at[t, r], t, XROW, (row_peer(off), c))

        @pl.loop(1, plane)
        def _(off):
            send(xs.at[t, c], xs.at[t, c], t, XOWN, (r, z * plane + plane_peer(off)))

        await_bytes(xs.at[t, pl.ds(0, 1)], recv_sem.at[t, XZ])

        @pl.loop(1, plane)
        def _(off):
            send(xs.at[t, partner], xs.at[t, partner], t, XOTHER, (r, z * plane + plane_peer(off)))

    def densify():
        for i in range(parts):
            tile_copy(i).wait()

        def add(i, total):
            total = raw[idx[0, i]].astype(F32) + total * idx[1, i].astype(F32)
            run[i] = total.astype(BF16)
            return total

        lax.fori_loop(0, slots, add, jnp.zeros((blk, blk), F32), unroll=4)

        @pl.loop(0, n_col)
        def _(cb):
            for rb in range(n_row):
                p = rb * n_col + cb
                dense[cb, rb * blk : (rb + 1) * blk, :] = run[idx[2, p]] * idx[3, p].astype(BF16)

    def transposed(t, half, slot, kind):
        down = jnp.concatenate([ys[t, i] for i in range(n_row)], axis=1)

        def pair(g):
            first = half * plane + plane_peer(2 * g)
            second = half * plane + plane_peer(2 * g + 1)
            a = jnp.concatenate([dense[first], dense[second]], axis=1)
            return jnp.dot(down, a, preferred_element_type=F32).astype(BF16)

        def ship(off):
            send(
                bstage.at[slot, off],
                bland.at[t, slot, off - 1],
                t,
                kind,
                (r, z * plane + plane_peer(off)),
            )

        part = pair(0)
        bland[t, slot, plane - 1] = part[:, :blk]
        bstage[slot, 1] = part[:, blk:]
        ship(1)

        @pl.loop(1, plane // 2)
        def _(g):
            part = pair(g)
            bstage[slot, 2 * g] = part[:, :blk]
            bstage[slot, 2 * g + 1] = part[:, blk:]
            ship(2 * g)
            ship(2 * g + 1)

    def forward(t, half, last):
        @pl.loop(0, n_row // 2)
        def _(m):
            rows = pl.ds(pl.multiple_of(m * 2 * blk, 2 * blk), 2 * blk)
            total = facc[m] if last else jnp.zeros(facc.shape[1:], F32)
            for p in range(plane // 2):
                at = half * plane + 2 * p
                a = jnp.concatenate([dense[at, rows, :], dense[at + 1, rows, :]], axis=1)
                v = jnp.concatenate([xs[t, at], xs[t, at + 1]], axis=1)
                total = total + lax.dot_general(a, v, LAST, preferred_element_type=F32)
            if last:
                total = total.T.astype(BF16)
                fstage[2 * m] = total[:, :blk]
                fstage[2 * m + 1] = total[:, blk:]
            else:
                facc[m] = total

    def total_of(land, t, count):
        total = land[t, 0].astype(F32)
        for i in range(1, count):
            total = total + land[t, i].astype(F32)
        return total

    def term(t):
        other = (z + 1) % 2
        await_bytes(ys.at[t, pl.ds(0, n_row - 1)], recv_sem.at[t, XROW])
        transposed(t, other, 0, POTHER)
        transposed(t, z, 1, POWN)
        await_bytes(xs.at[t, pl.ds(0, plane - 1)], recv_sem.at[t, XOWN])
        forward(t, z, False)
        await_bytes(xs.at[t, pl.ds(0, plane - 1)], recv_sem.at[t, XOTHER])
        forward(t, other, True)
        fland[t, n_row - 1] = fstage[r]

        @pl.loop(1, n_row)
        def _(off):
            to = row_peer(off)
            send(fstage.at[to], fland.at[t, off - 1], t, PROW, (to, c))

        await_bytes(bland.at[t, 0, pl.ds(0, plane - 1)], recv_sem.at[t, POTHER])
        zstage[...] = total_of(bland.at[:, 0], t, plane)
        send(zstage, zland.at[t], t, PZ, (r, partner))
        await_bytes(bland.at[t, 1, pl.ds(0, plane - 1)], recv_sem.at[t, POWN])
        total = total_of(bland.at[:, 1], t, plane)
        await_bytes(fland.at[t, pl.ds(0, n_row - 1)], recv_sem.at[t, PROW])
        total = total + total_of(fland, t, n_row)
        await_bytes(zland.at[t], recv_sem.at[t, PZ])
        total = total + zland[t]
        score[...] = beta_t[...] * total + seeds_t[...]

        await_bytes(xs.at[t, pl.ds(0, 1)], send_sem.at[t, XZ])
        await_bytes(ys.at[t, pl.ds(0, n_row - 1)], send_sem.at[t, XROW])
        await_bytes(xs.at[t, pl.ds(0, plane - 1)], send_sem.at[t, XOWN])
        await_bytes(xs.at[t, pl.ds(0, plane - 1)], send_sem.at[t, XOTHER])
        await_bytes(bland.at[t, 0, pl.ds(0, plane - 1)], send_sem.at[t, POTHER])
        await_bytes(bland.at[t, 1, pl.ds(0, plane - 1)], send_sem.at[t, POWN])
        await_bytes(fland.at[t, pl.ds(0, n_row - 1)], send_sem.at[t, PROW])
        await_bytes(zland.at[t], send_sem.at[t, PZ])

    spread(0)
    densify()

    @pl.loop(0, TERMS - 1)
    def _(t):
        term(t)
        spread(t + 1)

    term(TERMS - 1)
    out[...] = score[...].T


def order_of(block_rows, block_cols, live, n_row, n_col):
    slots = block_rows.shape[0]
    every = jnp.arange(slots, dtype=jnp.int32)
    places = jnp.arange(n_row * n_col, dtype=jnp.int32)
    key = jnp.where(every < live, block_rows * n_col + block_cols, n_row * n_col)
    unique = key * slots + every
    rank = jnp.sum((unique[None, :] < unique[:, None]).astype(jnp.int32), axis=1)
    hit = rank[:, None] == every[None, :]
    order = jnp.sum(jnp.where(hit, every[:, None], 0), axis=0)
    keys = jnp.sum(jnp.where(hit, key[:, None], 0), axis=0)
    goes_on = jnp.concatenate([jnp.zeros((1,), jnp.int32), (keys[1:] == keys[:-1]).astype(jnp.int32)])
    upto = jnp.sum((key[:, None] <= places[None, :]).astype(jnp.int32), axis=0)
    there = jnp.sum((key[:, None] == places[None, :]).astype(jnp.int32), axis=0)
    ends = jnp.stack([jnp.maximum(upto - 1, 0), (there > 0).astype(jnp.int32)])
    return jnp.concatenate([jnp.stack([order, goes_on]), ends])


def shards(n_row, n_col, side, tiles, block_rows, block_cols, live, seeds, beta):
    tiles = tiles[0, 0]
    slots, blk, _ = tiles.shape
    width = seeds.shape[1]
    plane = side * side
    idx = order_of(block_rows[0, 0], block_cols[0, 0], live[0, 0], n_row, n_col)
    vmem = pl.BlockSpec(memory_space=pltpu.VMEM)
    return pl.pallas_call(
        functools.partial(kernel, side),
        out_shape=jax.ShapeDtypeStruct(seeds.shape, F32),
        in_specs=[
            pl.BlockSpec(memory_space=pltpu.SMEM),
            pl.BlockSpec(memory_space=pl.ANY),
            vmem,
            vmem,
        ],
        out_specs=vmem,
        scratch_shapes=[
            pltpu.VMEM((slots, blk, blk), BF16),
            pltpu.VMEM((slots, blk, blk), BF16),
            pltpu.VMEM((n_col, n_row * blk, blk), BF16),
            pltpu.VMEM((TERMS, n_col, width, blk), BF16),
            pltpu.VMEM((TERMS, n_row, width, blk), BF16),
            pltpu.VMEM((2, plane, width, blk), BF16),
            pltpu.VMEM((n_row, width, blk), BF16),
            pltpu.VMEM((TERMS, 2, plane, width, blk), BF16),
            pltpu.VMEM((TERMS, n_row, width, blk), BF16),
            pltpu.VMEM((width, blk), F32),
            pltpu.VMEM((TERMS, width, blk), F32),
            pltpu.VMEM((n_row // 2, 2 * blk, width), F32),
            pltpu.VMEM((width, blk), F32),
            pltpu.VMEM((width, blk), F32),
            pltpu.VMEM((width, blk), F32),
            pltpu.SemaphoreType.DMA((4,)),
            pltpu.SemaphoreType.DMA((TERMS, 8)),
            pltpu.SemaphoreType.DMA((TERMS, 8)),
        ],
        compiler_params=pltpu.CompilerParams(
            collective_id=0, has_side_effects=True, vmem_limit_bytes=56 << 20
        ),
        cost_estimate=pl.CostEstimate(
            flops=TERMS * 4 * n_row * n_col * blk * blk * width,
            bytes_accessed=2 * slots * blk * blk,
            transcendentals=0,
        ),
    )(idx, tiles, seeds, beta[None, :])


def solution(mesh):
    n_row, n_col = mesh.shape["row"], mesh.shape["col"]
    side = 1
    while 2 * side * side < n_col:
        side *= 2
    placed = (
        P("row", "col", None, None, None),
        P("row", "col", None),
        P("row", "col", None),
        P("row", "col"),
        P(("col", "row"), None),
        P(),
    )
    return jax.shard_map(
        functools.partial(shards, n_row, n_col, side),
        mesh=mesh,
        in_specs=placed,
        out_specs=P(("col", "row"), None),
        check_vma=False,
    )
```

```python
import functools

import jax
import jax.numpy as jnp
from jax import lax
from jax.experimental import pallas as pl
from jax.experimental.pallas import tpu as pltpu
from jax.sharding import PartitionSpec as P

TERMS = 4
MESH = pl.DeviceIdType.MESH
F32 = jnp.float32
BF16 = jnp.bfloat16
LAST = (((1,), (1,)), ((), ()))

XZ, XOWN, XOTHER, XSIB, XNEAR, XFAR, POTHER, POWN, PROW, PZ = range(10)


def far_first(side):
    steps = [(dy, dx) for dy in range(side) for dx in range(side)]
    return sorted(steps, key=lambda s: -min(s[0], side - s[0]) - min(s[1], side - s[1]))


def kernel(
    idx,
    tiles,
    seeds,
    beta,
    out,
    raw,
    run,
    dense,
    xs,
    ys,
    bacc,
    bstage,
    fstage,
    bland,
    fland,
    zstage,
    zland,
    facc,
    beta_t,
    score,
    tile_sem,
    send_sem,
    recv_sem,
):
    slots, blk, _ = raw.shape
    n_row = ys.shape[1]
    chips = n_row // 2
    plane = bstage.shape[1]
    side = round(plane**0.5)
    n_col = 2 * plane
    parts = tile_sem.shape[0]
    chunk = slots // parts
    steps = far_first(side)
    r = lax.axis_index("row")
    c = lax.axis_index("col")
    high, core = r // 2, r % 2
    sibling = (core + 1) % 2
    z = c // plane
    y = (c % plane) // side
    x = c % side
    other = (z + 1) % 2
    yx = y * side + x

    def stepped(i):
        dy, dx = steps[i]
        return ((y + dy) % side) * side + (x + dx) % side

    def chip(k):
        return (high + k) % chips

    def rows_of(k):
        return pl.ds(pl.multiple_of(chip(k) * 2 * blk, 2 * blk), 2 * blk)

    def tile_copy(i):
        part = pl.ds(i * chunk, chunk)
        return pltpu.make_async_copy(tiles.at[part], raw.at[part], tile_sem.at[i])

    for i in range(parts):
        tile_copy(i).start()

    def send(src, dst, t, kind, device):
        pltpu.make_async_remote_copy(
            src_ref=src,
            dst_ref=dst,
            send_sem=send_sem.at[t, kind],
            recv_sem=recv_sem.at[t, kind],
            device_id=device,
            device_id_type=MESH,
        ).start()

    def moved(t, kind):
        if kind in (XOWN, XOTHER, POTHER, POWN):
            return bland.at[t, 0, pl.ds(0, plane - 1)]
        if kind == PZ:
            return zland.at[t]
        count = {XZ: 1, XSIB: 1, XFAR: 2, XNEAR: n_row - 4, PROW: n_row - 1}[kind]
        return fland.at[t, pl.ds(0, count)]

    def arrived(t, kind):
        ref = moved(t, kind)
        pltpu.make_async_copy(ref, ref, recv_sem.at[t, kind]).wait()

    def left(t, kind):
        ref = moved(t, kind)
        pltpu.make_async_copy(ref, ref, send_sem.at[t, kind]).wait()

    barrier = pltpu.get_barrier_semaphore()

    def greet(device):
        pl.semaphore_signal(barrier, inc=1, device_id=device, device_id_type=MESH)

    for off in range(1, n_row):
        greet(((r + off) % n_row, c))
    for i in range(plane - 1):
        greet((r, z * plane + stepped(i)))
    greet((r, other * plane + yx))

    def add_slots():
        for i in range(parts):
            tile_copy(i).wait()

        def add(i, total):
            total = raw[idx[0, i]].astype(F32) + total * idx[1, i].astype(F32)
            run[i] = total.astype(BF16)
            return total

        lax.fori_loop(0, slots, add, jnp.zeros((blk, blk), F32), unroll=4)

    def place():
        @pl.loop(0, n_col)
        def _(cb):
            for rb in range(n_row):
                p = rb * n_col + cb
                dense[cb, rb * blk : (rb + 1) * blk, :] = run[idx[2, p]] * idx[3, p].astype(BF16)

    def spread(t):
        current = score[...].astype(BF16)
        ys[t, r] = current
        xs[t, c] = current
        piece = ys.at[t, r]
        for k in sorted(range(1, chips), key=lambda k: -min(k, chips - k)):
            kind = XFAR if 2 * k == chips else XNEAR
            for to in range(2):
                send(piece, piece, t, kind, (2 * chip(k) + to, c))
        send(piece, piece, t, XSIB, (2 * high + sibling, c))
        piece = xs.at[t, c]
        send(piece, piece, t, XZ, (r, other * plane + yx))
        for i in range(plane - 1):
            send(piece, piece, t, XOWN, (r, z * plane + stepped(i)))

    def pass_on(t):
        arrived(t, XZ)
        piece = xs.at[t, other * plane + yx]
        for i in range(plane - 1):
            send(piece, piece, t, XOTHER, (r, z * plane + stepped(i)))

    def pair(zz, g):
        return zz * plane + stepped(2 * g), zz * plane + stepped(2 * g + 1)

    def down(t, ks):
        return jnp.concatenate([ys[t, 2 * chip(k) + i] for k in ks for i in range(2)], axis=1)

    def block(zz, g, ks):
        one, two = pair(zz, g)
        both = [jnp.concatenate([dense[one, rows_of(k), :], dense[two, rows_of(k), :]], axis=1) for k in ks]
        return jnp.concatenate(both, axis=0)

    def transposed(t, ks, first):
        v = down(t, ks)
        for slot, zz in enumerate((other, z)):
            for g in range(plane // 2):
                part = jnp.dot(v, block(zz, g, ks), preferred_element_type=F32)
                bacc[slot, g] = part if first else bacc[slot, g] + part

    def transposed_last(t, ks):
        v = down(t, ks)
        for slot, zz, kind in ((0, other, POTHER), (1, z, POWN)):
            for g in range(plane // 2):
                part = jnp.dot(v, block(zz, g, ks), preferred_element_type=F32)
                part = (bacc[slot, g] + part).astype(BF16)
                bstage[slot, 2 * g] = part[:, :blk]
                bstage[slot, 2 * g + 1] = part[:, blk:]
                for i in (2 * g, 2 * g + 1):
                    if i < plane - 1:
                        send(bstage.at[slot, i], bland.at[t, slot, i], t, kind, (r, z * plane + stepped(i)))

    def forward(t, zz, last):
        for m, k in enumerate(sorted(range(chips), key=lambda k: -min(k, chips - k))):
            total = facc[m] if last else jnp.zeros(facc.shape[1:], F32)
            for p in range(plane // 2):
                at = zz * plane + 2 * p
                a = jnp.concatenate([dense[at, rows_of(k), :], dense[at + 1, rows_of(k), :]], axis=1)
                v = jnp.concatenate([xs[t, at], xs[t, at + 1]], axis=1)
                total = total + lax.dot_general(a, v, LAST, preferred_element_type=F32)
            if not last:
                facc[m] = total
                continue
            total = total.T.astype(BF16)
            fstage[2 * m] = total[:, :blk]
            fstage[2 * m + 1] = total[:, blk:]
            if k:
                for to in range(2):
                    send(fstage.at[2 * m + to], fland.at[t, 2 * m + core], t, PROW, (2 * chip(k) + to, c))
            else:
                send(fstage.at[2 * m + sibling], fland.at[t, 2 * m], t, PROW, (2 * high + sibling, c))

    def total_of(land, t, count, total):
        for i in range(count):
            total = total + land[t, i].astype(F32)
        return total

    beta_t[...] = jnp.broadcast_to(beta[...], (blk, beta.shape[1])).T
    score[...] = seeds[...]
    add_slots()
    pl.semaphore_wait(barrier, (n_row - 1) + (plane - 1) + 1)
    spread(0)
    place()

    @pl.loop(0, TERMS)
    def _(t):
        arrived(t, XSIB)
        transposed(t, (0,), True)
        pass_on(t)
        near = tuple(k for k in range(1, chips) if 2 * k != chips)
        if near:
            arrived(t, XNEAR)
            transposed(t, near, False)
        arrived(t, XFAR)
        transposed_last(t, (chips // 2,))
        arrived(t, XOWN)
        forward(t, z, False)
        arrived(t, XOTHER)
        forward(t, other, True)
        arrived(t, POTHER)
        zstage[...] = total_of(bland.at[:, 0], t, plane - 1, bstage[0, plane - 1].astype(F32))
        send(zstage, zland.at[t], t, PZ, (r, other * plane + yx))
        arrived(t, POWN)
        total = total_of(bland.at[:, 1], t, plane - 1, bstage[1, plane - 1].astype(F32))
        arrived(t, PROW)
        total = total_of(fland, t, n_row - 1, total + fstage[n_row - 2 + core].astype(F32))
        arrived(t, PZ)
        total = total + zland[t]
        score[...] = beta_t[...] * total + seeds[...]

        for kind in range(10):
            if kind != XNEAR or near:
                left(t, kind)

        @pl.when(t < TERMS - 1)
        def _():
            spread(t + 1)

    out[...] = score[...]


def order_of(block_rows, block_cols, live, n_row, n_col):
    slots = block_rows.shape[0]
    every = jnp.arange(slots, dtype=jnp.int32)
    places = jnp.arange(n_row * n_col, dtype=jnp.int32)
    key = jnp.where(every < live, block_rows * n_col + block_cols, n_row * n_col)
    unique = key * slots + every
    rank = jnp.sum((unique[None, :] < unique[:, None]).astype(jnp.int32), axis=1)
    hit = rank[:, None] == every[None, :]
    order = jnp.sum(jnp.where(hit, every[:, None], 0), axis=0)
    keys = jnp.sum(jnp.where(hit, key[:, None], 0), axis=0)
    goes_on = jnp.concatenate([jnp.zeros((1,), jnp.int32), (keys[1:] == keys[:-1]).astype(jnp.int32)])
    upto = jnp.sum((key[:, None] <= places[None, :]).astype(jnp.int32), axis=0)
    there = jnp.sum((key[:, None] == places[None, :]).astype(jnp.int32), axis=0)
    ends = jnp.stack([jnp.maximum(upto - 1, 0), (there > 0).astype(jnp.int32)])
    return jnp.concatenate([jnp.stack([order, goes_on]), ends])


def shards(n_row, n_col, tiles, block_rows, block_cols, live, seeds, beta):
    tiles = tiles[0, 0]
    slots, blk, _ = tiles.shape
    width = seeds.shape[1]
    plane = n_col // 2
    idx = order_of(block_rows[0, 0], block_cols[0, 0], live[0, 0], n_row, n_col)
    vmem = pl.BlockSpec(memory_space=pltpu.VMEM)
    scores = pl.pallas_call(
        kernel,
        out_shape=jax.ShapeDtypeStruct((width, blk), F32),
        in_specs=[
            pl.BlockSpec(memory_space=pltpu.SMEM),
            pl.BlockSpec(memory_space=pl.ANY),
            vmem,
            vmem,
        ],
        out_specs=vmem,
        scratch_shapes=[
            pltpu.VMEM((slots, blk, blk), BF16),
            pltpu.VMEM((slots, blk, blk), BF16),
            pltpu.VMEM((n_col, n_row * blk, blk), BF16),
            pltpu.VMEM((TERMS, n_col, width, blk), BF16),
            pltpu.VMEM((TERMS, n_row, width, blk), BF16),
            pltpu.VMEM((2, plane // 2, width, 2 * blk), F32),
            pltpu.VMEM((2, plane, width, blk), BF16),
            pltpu.VMEM((n_row, width, blk), BF16),
            pltpu.VMEM((TERMS, 2, plane - 1, width, blk), BF16),
            pltpu.VMEM((TERMS, n_row - 1, width, blk), BF16),
            pltpu.VMEM((width, blk), F32),
            pltpu.VMEM((TERMS, width, blk), F32),
            pltpu.VMEM((n_row // 2, 2 * blk, width), F32),
            pltpu.VMEM((width, blk), F32),
            pltpu.VMEM((width, blk), F32),
            pltpu.SemaphoreType.DMA((4,)),
            pltpu.SemaphoreType.DMA((TERMS, 10)),
            pltpu.SemaphoreType.DMA((TERMS, 10)),
        ],
        compiler_params=pltpu.CompilerParams(
            collective_id=0, has_side_effects=True, vmem_limit_bytes=56 << 20
        ),
        cost_estimate=pl.CostEstimate(
            flops=TERMS * 4 * n_row * n_col * blk * blk * width,
            bytes_accessed=2 * slots * blk * blk,
            transcendentals=0,
        ),
    )(idx, tiles, seeds.T, beta[None, :])
    return scores.T


def solution(mesh):
    n_row, n_col = mesh.shape["row"], mesh.shape["col"]
    placed = (
        P("row", "col", None, None, None),
        P("row", "col", None),
        P("row", "col", None),
        P("row", "col"),
        P(("col", "row"), None),
        P(),
    )
    return jax.shard_map(
        functools.partial(shards, n_row, n_col),
        mesh=mesh,
        in_specs=placed,
        out_specs=P(("col", "row"), None),
        check_vma=False,
    )
```

```python
import functools

import jax
import jax.numpy as jnp
from jax import lax
from jax.experimental import pallas as pl
from jax.experimental.pallas import tpu as pltpu
from jax.sharding import PartitionSpec as P

TERMS = 4
MESH = pl.DeviceIdType.MESH
F32 = jnp.float32
BF16 = jnp.bfloat16
LAST = (((1,), (1,)), ((), ()))

XZ, XOWN, XOTHER, XSIB, XNEAR, XFAR, POTHER, POWN, PROW, PZ = range(10)


def far_first(side):
    steps = [(dy, dx) for dy in range(side) for dx in range(side)]
    return sorted(steps, key=lambda s: -min(s[0], side - s[0]) - min(s[1], side - s[1]))


def kernel(
    live,
    block_rows,
    block_cols,
    tiles,
    seeds,
    beta,
    out,
    raw,
    run,
    dense,
    xs,
    ys,
    bacc,
    bstage,
    fstage,
    bland,
    fland,
    zstage,
    zland,
    facc,
    beta_t,
    score,
    table,
    idx,
    table_sem,
    tile_sem,
    send_sem,
    recv_sem,
):
    slots, blk, _ = raw.shape
    n_row = ys.shape[1]
    chips = n_row // 2
    plane = bstage.shape[1]
    side = round(plane**0.5)
    n_col = 2 * plane
    parts = tile_sem.shape[0]
    chunk = slots // parts
    steps = far_first(side)
    r = lax.axis_index("row")
    c = lax.axis_index("col")
    high, core = r // 2, r % 2
    sibling = (core + 1) % 2
    z = c // plane
    y = (c % plane) // side
    x = c % side
    other = (z + 1) % 2
    yx = y * side + x

    def stepped(i):
        dy, dx = steps[i]
        return ((y + dy) % side) * side + (x + dx) % side

    def chip(k):
        return (high + k) % chips

    def rows_of(k):
        return pl.ds(pl.multiple_of(chip(k) * 2 * blk, 2 * blk), 2 * blk)

    def tile_copy(i):
        part = pl.ds(i * chunk, chunk)
        return pltpu.make_async_copy(tiles.at[part], raw.at[part], tile_sem.at[i])

    for i in range(parts):
        tile_copy(i).start()

    def send(src, dst, t, kind, device):
        pltpu.make_async_remote_copy(
            src_ref=src,
            dst_ref=dst,
            send_sem=send_sem.at[t, kind],
            recv_sem=recv_sem.at[t, kind],
            device_id=device,
            device_id_type=MESH,
        ).start()

    def moved(t, kind):
        if kind in (XOWN, XOTHER, POTHER, POWN):
            return bland.at[t, 0, pl.ds(0, plane - 1)]
        if kind == PZ:
            return zland.at[t]
        count = {XZ: 1, XSIB: 1, XFAR: 2, XNEAR: n_row - 4, PROW: n_row - 1}[kind]
        return fland.at[t, pl.ds(0, count)]

    def arrived(t, kind):
        ref = moved(t, kind)
        pltpu.make_async_copy(ref, ref, recv_sem.at[t, kind]).wait()

    def left(t, kind):
        ref = moved(t, kind)
        pltpu.make_async_copy(ref, ref, send_sem.at[t, kind]).wait()

    barrier = pltpu.get_barrier_semaphore()

    def greet(device):
        pl.semaphore_signal(barrier, inc=1, device_id=device, device_id_type=MESH)

    for off in range(1, n_row):
        greet(((r + off) % n_row, c))
    for i in range(plane - 1):
        greet((r, z * plane + stepped(i)))
    greet((r, other * plane + yx))

    def order_slots():
        n = slots
        along = lax.broadcasted_iota(jnp.int32, (1, n), 1)
        key = jnp.where(along < live[...], block_rows[...] * n_col + block_cols[...], n_row * n_col)
        keys = jnp.broadcast_to(key, (n, n))
        keys_down = keys.T
        across = lax.broadcasted_iota(jnp.int32, (n, n), 1)
        down = lax.broadcasted_iota(jnp.int32, (n, n), 0)
        ahead = (keys_down < keys) | ((keys_down == keys) & (down < across))
        rank = jnp.sum(ahead.astype(jnp.int32), axis=0, keepdims=True)
        hit = jnp.broadcast_to(rank, (n, n)).T == across
        order = jnp.sum(jnp.where(hit, down, 0), axis=0, keepdims=True)
        placed = jnp.sum(jnp.where(hit, keys_down, 0), axis=0, keepdims=True)
        goes_on = (placed == pltpu.roll(placed, 1, axis=1)) & (along > 0)
        upto = jnp.sum((keys_down <= across).astype(jnp.int32), axis=0, keepdims=True)
        there = jnp.sum((keys_down == across).astype(jnp.int32), axis=0, keepdims=True)
        table[0:1, :] = order
        table[1:2, :] = goes_on.astype(jnp.int32)
        table[2:3, :] = jnp.maximum(upto - 1, 0)
        table[3:4, :] = (there > 0).astype(jnp.int32)
        copy = pltpu.make_async_copy(table, idx, table_sem)
        copy.start()
        copy.wait()

    def add_slots():
        for i in range(parts):
            tile_copy(i).wait()

        def add(i, total):
            total = raw[idx[0, i]].astype(F32) + total * idx[1, i].astype(F32)
            run[i] = total.astype(BF16)
            return total

        lax.fori_loop(0, slots, add, jnp.zeros((blk, blk), F32), unroll=4)

    def place():
        @pl.loop(0, n_col)
        def _(cb):
            for rb in range(n_row):
                p = rb * n_col + cb
                dense[cb, rb * blk : (rb + 1) * blk, :] = run[idx[2, p]] * idx[3, p].astype(BF16)

    def spread(t):
        current = score[...].astype(BF16)
        ys[t, r] = current
        xs[t, c] = current
        piece = xs.at[t, c]
        send(piece, piece, t, XZ, (r, other * plane + yx))
        piece = ys.at[t, r]
        for k in sorted(range(1, chips), key=lambda k: -min(k, chips - k)):
            kind = XFAR if 2 * k == chips else XNEAR
            for to in range(2):
                send(piece, piece, t, kind, (2 * chip(k) + to, c))
        send(piece, piece, t, XSIB, (2 * high + sibling, c))
        piece = xs.at[t, c]
        for i in range(plane - 1):
            send(piece, piece, t, XOWN, (r, z * plane + stepped(i)))

    def pass_on(t):
        arrived(t, XZ)
        piece = xs.at[t, other * plane + yx]
        for i in range(plane - 1):
            send(piece, piece, t, XOTHER, (r, z * plane + stepped(i)))

    def pair(zz, g):
        return zz * plane + stepped(2 * g), zz * plane + stepped(2 * g + 1)

    def down(t, ks):
        return jnp.concatenate([ys[t, 2 * chip(k) + i] for k in ks for i in range(2)], axis=1)

    def block(zz, g, ks):
        one, two = pair(zz, g)
        both = [jnp.concatenate([dense[one, rows_of(k), :], dense[two, rows_of(k), :]], axis=1) for k in ks]
        return jnp.concatenate(both, axis=0)

    def transposed(t, planes, ks, first):
        v = down(t, ks)
        for slot, zz in planes:
            for g in range(plane // 2):
                part = jnp.dot(v, block(zz, g, ks), preferred_element_type=F32)
                bacc[slot, g] = part if first else bacc[slot, g] + part

    def transposed_last(t, slot, zz, ks, kind):
        v = down(t, ks)
        for g in range(plane // 2):
            part = jnp.dot(v, block(zz, g, ks), preferred_element_type=F32)
            part = (bacc[slot, g] + part).astype(BF16)
            bstage[slot, 2 * g] = part[:, :blk]
            bstage[slot, 2 * g + 1] = part[:, blk:]
            for i in (2 * g, 2 * g + 1):
                if i < plane - 1:
                    send(bstage.at[slot, i], bland.at[t, slot, i], t, kind, (r, z * plane + stepped(i)))

    def forward(t, zz, last):
        for m, k in enumerate(sorted(range(chips), key=lambda k: -min(k, chips - k))):
            total = facc[m] if last else jnp.zeros(facc.shape[1:], F32)
            for p in range(plane // 2):
                at = zz * plane + 2 * p
                a = jnp.concatenate([dense[at, rows_of(k), :], dense[at + 1, rows_of(k), :]], axis=1)
                v = jnp.concatenate([xs[t, at], xs[t, at + 1]], axis=1)
                total = total + lax.dot_general(a, v, LAST, preferred_element_type=F32)
            if not last:
                facc[m] = total
                continue
            total = total.T.astype(BF16)
            fstage[2 * m] = total[:, :blk]
            fstage[2 * m + 1] = total[:, blk:]
            if k:
                for to in range(2):
                    send(fstage.at[2 * m + to], fland.at[t, 2 * m + core], t, PROW, (2 * chip(k) + to, c))
            else:
                send(fstage.at[2 * m + sibling], fland.at[t, 2 * m], t, PROW, (2 * high + sibling, c))

    def total_of(land, t, count, total):
        for i in range(count):
            total = total + land[t, i].astype(F32)
        return total

    def begin(t):
        arrived(t, XSIB)
        transposed(t, ((0, other), (1, z)), (0,), True)

    beta_t[...] = jnp.broadcast_to(beta[...], (blk, beta.shape[1])).T
    score[...] = seeds[...]
    pl.semaphore_wait(barrier, (n_row - 1) + (plane - 1) + 1)
    spread(0)
    order_slots()
    add_slots()
    pass_on(0)
    place()
    begin(0)

    @pl.loop(0, TERMS)
    def _(t):
        near = tuple(k for k in range(1, chips) if 2 * k != chips)
        if near:
            arrived(t, XNEAR)
            transposed(t, ((0, other), (1, z)), near, False)
        arrived(t, XFAR)
        transposed_last(t, 0, other, (chips // 2,), POTHER)
        transposed_last(t, 1, z, (chips // 2,), POWN)
        arrived(t, XOWN)
        forward(t, z, False)
        arrived(t, XOTHER)
        forward(t, other, True)
        arrived(t, POTHER)
        crossing = total_of(bland.at[:, 0], t, plane - 1, bstage[0, plane - 1].astype(F32))
        zstage[...] = crossing.astype(BF16)
        send(zstage, zland.at[t], t, PZ, (r, other * plane + yx))
        arrived(t, POWN)
        total = total_of(bland.at[:, 1], t, plane - 1, bstage[1, plane - 1].astype(F32))
        arrived(t, PROW)
        total = total_of(fland, t, n_row - 1, total + fstage[n_row - 2 + core].astype(F32))
        arrived(t, PZ)
        total = total + zland[t].astype(F32)
        score[...] = beta_t[...] * total + seeds[...]

        @pl.when(t < TERMS - 1)
        def _():
            spread(t + 1)
            begin(t + 1)
            pass_on(t + 1)

        for kind in range(10):
            if kind != XNEAR or near:
                left(t, kind)

    out[...] = score[...]


def shards(n_row, n_col, tiles, block_rows, block_cols, live, seeds, beta):
    tiles = tiles[0, 0]
    slots, blk, _ = tiles.shape
    width = seeds.shape[1]
    plane = n_col // 2
    assert slots == n_row * n_col
    vmem = pl.BlockSpec(memory_space=pltpu.VMEM)
    scores = pl.pallas_call(
        kernel,
        out_shape=jax.ShapeDtypeStruct((width, blk), F32),
        in_specs=[
            vmem,
            vmem,
            vmem,
            pl.BlockSpec(memory_space=pl.ANY),
            vmem,
            vmem,
        ],
        out_specs=vmem,
        scratch_shapes=[
            pltpu.VMEM((slots, blk, blk), BF16),
            pltpu.VMEM((slots, blk, blk), BF16),
            pltpu.VMEM((n_col, n_row * blk, blk), BF16),
            pltpu.VMEM((TERMS, n_col, width, blk), BF16),
            pltpu.VMEM((TERMS, n_row, width, blk), BF16),
            pltpu.VMEM((2, plane // 2, width, 2 * blk), F32),
            pltpu.VMEM((2, plane, width, blk), BF16),
            pltpu.VMEM((n_row, width, blk), BF16),
            pltpu.VMEM((TERMS, 2, plane - 1, width, blk), BF16),
            pltpu.VMEM((TERMS, n_row - 1, width, blk), BF16),
            pltpu.VMEM((width, blk), BF16),
            pltpu.VMEM((TERMS, width, blk), BF16),
            pltpu.VMEM((n_row // 2, 2 * blk, width), F32),
            pltpu.VMEM((width, blk), F32),
            pltpu.VMEM((width, blk), F32),
            pltpu.VMEM((8, slots), jnp.int32),
            pltpu.SMEM((8, slots), jnp.int32),
            pltpu.SemaphoreType.DMA,
            pltpu.SemaphoreType.DMA((4,)),
            pltpu.SemaphoreType.DMA((TERMS, 10)),
            pltpu.SemaphoreType.DMA((TERMS, 10)),
        ],
        compiler_params=pltpu.CompilerParams(
            collective_id=0, has_side_effects=True, vmem_limit_bytes=56 << 20
        ),
        cost_estimate=pl.CostEstimate(
            flops=TERMS * 4 * n_row * n_col * blk * blk * width,
            bytes_accessed=2 * slots * blk * blk,
            transcendentals=0,
        ),
    )(live, block_rows[0], block_cols[0], tiles, seeds.T, beta[None, :])
    return scores.T


def solution(mesh):
    n_row, n_col = mesh.shape["row"], mesh.shape["col"]
    placed = (
        P("row", "col", None, None, None),
        P("row", "col", None),
        P("row", "col", None),
        P("row", "col"),
        P(("col", "row"), None),
        P(),
    )
    return jax.shard_map(
        functools.partial(shards, n_row, n_col),
        mesh=mesh,
        in_specs=placed,
        out_specs=P(("col", "row"), None),
        check_vma=False,
    )
```

```python
import functools

import jax
import jax.numpy as jnp
from jax import lax
from jax.experimental import pallas as pl
from jax.experimental.pallas import tpu as pltpu
from jax.sharding import PartitionSpec as P

TERMS = 4
MESH = pl.DeviceIdType.MESH
F32 = jnp.float32
BF16 = jnp.bfloat16
LAST = (((1,), (1,)), ((), ()))

XZ, XOWN, XOTHER, XSIB, XNEAR, XFAR, POTHER, POWN, PROW, PZ = range(10)


def far_first(side):
    steps = [(dy, dx) for dy in range(side) for dx in range(side)]
    return sorted(steps, key=lambda s: (-min(s[0], side - s[0]) - min(s[1], side - s[1]), 0 in s))


def kernel(
    live,
    block_rows,
    block_cols,
    tiles,
    seeds,
    beta,
    out,
    raw,
    run,
    dense,
    xs,
    ys,
    bacc,
    bstage,
    fstage,
    bland,
    fland,
    zstage,
    zland,
    facc,
    beta_t,
    score,
    table,
    idx,
    table_sem,
    tile_sem,
    send_sem,
    recv_sem,
):
    slots, blk, _ = raw.shape
    n_row = ys.shape[1]
    chips = n_row // 2
    plane = bstage.shape[1]
    side = round(plane**0.5)
    n_col = 2 * plane
    parts = tile_sem.shape[0]
    chunk = slots // parts
    steps = far_first(side)
    r = lax.axis_index("row")
    c = lax.axis_index("col")
    high, core = r // 2, r % 2
    sibling = (core + 1) % 2
    z = c // plane
    y = (c % plane) // side
    x = c % side
    other = (z + 1) % 2
    yx = y * side + x

    def stepped(i):
        dy, dx = steps[i]
        return ((y + dy) % side) * side + (x + dx) % side

    def chip(k):
        return (high + k) % chips

    def rows_of(k):
        return pl.ds(pl.multiple_of(chip(k) * 2 * blk, 2 * blk), 2 * blk)

    def tile_copy(i):
        part = pl.ds(i * chunk, chunk)
        return pltpu.make_async_copy(tiles.at[part], raw.at[part], tile_sem.at[i])

    for i in range(parts):
        tile_copy(i).start()

    def send(src, dst, t, kind, device):
        pltpu.make_async_remote_copy(
            src_ref=src,
            dst_ref=dst,
            send_sem=send_sem.at[t, kind],
            recv_sem=recv_sem.at[t, kind],
            device_id=device,
            device_id_type=MESH,
        ).start()

    def moved(t, kind):
        if kind in (XOWN, XOTHER, POTHER, POWN):
            return bland.at[t, 0, pl.ds(0, plane - 1)]
        if kind == PZ:
            return zland.at[t]
        count = {XZ: 1, XSIB: 1, XFAR: 2, XNEAR: n_row - 4, PROW: n_row - 1}[kind]
        return fland.at[t, pl.ds(0, count)]

    def arrived(t, kind):
        ref = moved(t, kind)
        pltpu.make_async_copy(ref, ref, recv_sem.at[t, kind]).wait()

    def left(t, kind):
        ref = moved(t, kind)
        pltpu.make_async_copy(ref, ref, send_sem.at[t, kind]).wait()

    barrier = pltpu.get_barrier_semaphore()

    def greet(device):
        pl.semaphore_signal(barrier, inc=1, device_id=device, device_id_type=MESH)

    for off in range(1, n_row):
        greet(((r + off) % n_row, c))
    for i in range(plane - 1):
        greet((r, z * plane + stepped(i)))
    greet((r, other * plane + yx))

    def order_slots():
        n = slots
        along = lax.broadcasted_iota(jnp.int32, (1, n), 1)
        key = jnp.where(along < live[...], block_rows[...] * n_col + block_cols[...], n_row * n_col)
        keys = jnp.broadcast_to(key, (n, n))
        keys_down = keys.T
        across = lax.broadcasted_iota(jnp.int32, (n, n), 1)
        down = lax.broadcasted_iota(jnp.int32, (n, n), 0)
        ahead = (keys_down < keys) | ((keys_down == keys) & (down < across))
        rank = jnp.sum(ahead.astype(jnp.int32), axis=0, keepdims=True)
        hit = jnp.broadcast_to(rank, (n, n)).T == across
        order = jnp.sum(jnp.where(hit, down, 0), axis=0, keepdims=True)
        placed = jnp.sum(jnp.where(hit, keys_down, 0), axis=0, keepdims=True)
        goes_on = (placed == pltpu.roll(placed, 1, axis=1)) & (along > 0)
        upto = jnp.sum((keys_down <= across).astype(jnp.int32), axis=0, keepdims=True)
        there = jnp.sum((keys_down == across).astype(jnp.int32), axis=0, keepdims=True)
        table[0:1, :] = order
        table[1:2, :] = goes_on.astype(jnp.int32)
        table[2:3, :] = jnp.maximum(upto - 1, 0)
        table[3:4, :] = (there > 0).astype(jnp.int32)
        copy = pltpu.make_async_copy(table, idx, table_sem)
        copy.start()
        copy.wait()

    def add_slots():
        for i in range(parts):
            tile_copy(i).wait()

        def add(i, total):
            total = raw[idx[0, i]].astype(F32) + total * idx[1, i].astype(F32)
            run[i] = total.astype(BF16)
            return total

        lax.fori_loop(0, slots, add, jnp.zeros((blk, blk), F32), unroll=4)

    def place():
        @pl.loop(0, n_col)
        def _(cb):
            for rb in range(n_row):
                p = rb * n_col + cb
                dense[cb, rb * blk : (rb + 1) * blk, :] = run[idx[2, p]] * idx[3, p].astype(BF16)

    def spread(t):
        current = score[...].astype(BF16)
        ys[t, r] = current
        xs[t, c] = current
        piece = xs.at[t, c]
        send(piece, piece, t, XZ, (r, other * plane + yx))
        piece = ys.at[t, r]
        for k in sorted(range(1, chips), key=lambda k: -min(k, chips - k)):
            kind = XFAR if 2 * k == chips else XNEAR
            for to in range(2):
                send(piece, piece, t, kind, (2 * chip(k) + to, c))
        send(piece, piece, t, XSIB, (2 * high + sibling, c))
        piece = xs.at[t, c]
        for i in range(plane - 1):
            send(piece, piece, t, XOWN, (r, z * plane + stepped(i)))

    def pass_on(t):
        arrived(t, XZ)
        piece = xs.at[t, other * plane + yx]
        for i in range(plane - 1):
            send(piece, piece, t, XOTHER, (r, z * plane + stepped(i)))

    def pair(zz, g):
        return zz * plane + stepped(2 * g), zz * plane + stepped(2 * g + 1)

    def down(t, ks):
        return jnp.concatenate([ys[t, 2 * chip(k) + i] for k in ks for i in range(2)], axis=1)

    def block(zz, g, ks):
        one, two = pair(zz, g)
        both = [jnp.concatenate([dense[one, rows_of(k), :], dense[two, rows_of(k), :]], axis=1) for k in ks]
        return jnp.concatenate(both, axis=0)

    def transposed(t, planes, ks, first):
        v = down(t, ks)
        for slot, zz in planes:
            for g in range(plane // 2):
                part = jnp.dot(v, block(zz, g, ks), preferred_element_type=F32)
                bacc[slot, g] = part if first else bacc[slot, g] + part

    def transposed_last(t, slot, zz, ks, kind):
        v = down(t, ks)
        for g in range(plane // 2):
            part = jnp.dot(v, block(zz, g, ks), preferred_element_type=F32)
            part = (bacc[slot, g] + part).astype(BF16)
            bstage[slot, 2 * g] = part[:, :blk]
            bstage[slot, 2 * g + 1] = part[:, blk:]
            for i in (2 * g, 2 * g + 1):
                if slot == 0 and i < plane - 1:
                    send(bstage.at[slot, i], bland.at[t, slot, i], t, kind, (r, z * plane + stepped(i)))

    def ship_own(t, which):
        for i in which:
            send(bstage.at[1, i], bland.at[t, 1, i], t, POWN, (r, z * plane + stepped(i)))

    def forward(t, zz, last):
        for m, k in enumerate(sorted(range(chips), key=lambda k: -min(k, chips - k))):
            total = facc[m] if last else jnp.zeros(facc.shape[1:], F32)
            for p in range(plane // 2):
                at = zz * plane + 2 * p
                a = jnp.concatenate([dense[at, rows_of(k), :], dense[at + 1, rows_of(k), :]], axis=1)
                v = jnp.concatenate([xs[t, at], xs[t, at + 1]], axis=1)
                total = total + lax.dot_general(a, v, LAST, preferred_element_type=F32)
            if not last:
                facc[m] = total
                continue
            total = total.T.astype(BF16)
            fstage[2 * m] = total[:, :blk]
            fstage[2 * m + 1] = total[:, blk:]
            if k:
                for to in range(2):
                    send(fstage.at[2 * m + to], fland.at[t, 2 * m + core], t, PROW, (2 * chip(k) + to, c))
                if m == 0:
                    ship_own(t, range(plane - 1))
            else:
                send(fstage.at[2 * m + sibling], fland.at[t, 2 * m], t, PROW, (2 * high + sibling, c))

    def total_of(land, t, count, total):
        for i in range(count):
            total = total + land[t, i].astype(F32)
        return total

    def begin(t):
        arrived(t, XSIB)
        transposed(t, ((0, other), (1, z)), (0,), True)

    beta_t[...] = jnp.broadcast_to(beta[...], (blk, beta.shape[1])).T
    score[...] = seeds[...]
    pl.semaphore_wait(barrier, (n_row - 1) + (plane - 1) + 1)
    spread(0)
    order_slots()
    add_slots()
    pass_on(0)
    place()
    begin(0)

    @pl.loop(0, TERMS)
    def _(t):
        near = tuple(k for k in range(1, chips) if 2 * k != chips)
        if near:
            arrived(t, XNEAR)
            transposed(t, ((0, other), (1, z)), near, False)
        arrived(t, XFAR)
        transposed_last(t, 0, other, (chips // 2,), POTHER)
        arrived(t, XOWN)
        forward(t, z, False)
        transposed_last(t, 1, z, (chips // 2,), POWN)
        arrived(t, XOTHER)
        forward(t, other, True)
        arrived(t, POTHER)
        crossing = total_of(bland.at[:, 0], t, plane - 1, bstage[0, plane - 1].astype(F32))
        zstage[...] = crossing.astype(BF16)
        send(zstage, zland.at[t], t, PZ, (r, other * plane + yx))
        arrived(t, POWN)
        total = total_of(bland.at[:, 1], t, plane - 1, bstage[1, plane - 1].astype(F32))
        arrived(t, PROW)
        total = total_of(fland, t, n_row - 1, total + fstage[n_row - 2 + core].astype(F32))
        arrived(t, PZ)
        total = total + zland[t].astype(F32)
        score[...] = beta_t[...] * total + seeds[...]

        @pl.when(t < TERMS - 1)
        def _():
            spread(t + 1)
            begin(t + 1)
            pass_on(t + 1)

        for kind in range(10):
            if kind != XNEAR or near:
                left(t, kind)

    out[...] = score[...]


def shards(n_row, n_col, tiles, block_rows, block_cols, live, seeds, beta):
    tiles = tiles[0, 0]
    slots, blk, _ = tiles.shape
    width = seeds.shape[1]
    plane = n_col // 2
    assert slots == n_row * n_col
    vmem = pl.BlockSpec(memory_space=pltpu.VMEM)
    scores = pl.pallas_call(
        kernel,
        out_shape=jax.ShapeDtypeStruct((width, blk), F32),
        in_specs=[
            vmem,
            vmem,
            vmem,
            pl.BlockSpec(memory_space=pl.ANY),
            vmem,
            vmem,
        ],
        out_specs=vmem,
        scratch_shapes=[
            pltpu.VMEM((slots, blk, blk), BF16),
            pltpu.VMEM((slots, blk, blk), BF16),
            pltpu.VMEM((n_col, n_row * blk, blk), BF16),
            pltpu.VMEM((TERMS, n_col, width, blk), BF16),
            pltpu.VMEM((TERMS, n_row, width, blk), BF16),
            pltpu.VMEM((2, plane // 2, width, 2 * blk), F32),
            pltpu.VMEM((2, plane, width, blk), BF16),
            pltpu.VMEM((n_row, width, blk), BF16),
            pltpu.VMEM((TERMS, 2, plane - 1, width, blk), BF16),
            pltpu.VMEM((TERMS, n_row - 1, width, blk), BF16),
            pltpu.VMEM((width, blk), BF16),
            pltpu.VMEM((TERMS, width, blk), BF16),
            pltpu.VMEM((n_row // 2, 2 * blk, width), F32),
            pltpu.VMEM((width, blk), F32),
            pltpu.VMEM((width, blk), F32),
            pltpu.VMEM((8, slots), jnp.int32),
            pltpu.SMEM((8, slots), jnp.int32),
            pltpu.SemaphoreType.DMA,
            pltpu.SemaphoreType.DMA((4,)),
            pltpu.SemaphoreType.DMA((TERMS, 10)),
            pltpu.SemaphoreType.DMA((TERMS, 10)),
        ],
        compiler_params=pltpu.CompilerParams(
            collective_id=0, has_side_effects=True, vmem_limit_bytes=56 << 20
        ),
        cost_estimate=pl.CostEstimate(
            flops=TERMS * 4 * n_row * n_col * blk * blk * width,
            bytes_accessed=2 * slots * blk * blk,
            transcendentals=0,
        ),
    )(live, block_rows[0], block_cols[0], tiles, seeds.T, beta[None, :])
    return scores.T


def solution(mesh):
    n_row, n_col = mesh.shape["row"], mesh.shape["col"]
    placed = (
        P("row", "col", None, None, None),
        P("row", "col", None),
        P("row", "col", None),
        P("row", "col"),
        P(("col", "row"), None),
        P(),
    )
    return jax.shard_map(
        functools.partial(shards, n_row, n_col),
        mesh=mesh,
        in_specs=placed,
        out_specs=P(("col", "row"), None),
        check_vma=False,
    )
```

```python
import functools

import jax
import jax.numpy as jnp
from jax import lax
from jax.experimental import pallas as pl
from jax.experimental.pallas import tpu as pltpu
from jax.sharding import PartitionSpec as P

TERMS = 4
MESH = pl.DeviceIdType.MESH
F32 = jnp.float32
BF16 = jnp.bfloat16
LAST = (((1,), (1,)), ((), ()))

XZ, XOWN, XOTHER, XSIB, XNEAR, XFAR, POTHER, POWN, PROW, PZ = range(10)


def far_first(side):
    steps = [(dy, dx) for dy in range(side) for dx in range(side)]
    return sorted(steps, key=lambda s: (-min(s[0], side - s[0]) - min(s[1], side - s[1]), 0 in s))


def kernel(
    live,
    block_rows,
    block_cols,
    tiles,
    seeds,
    beta,
    out,
    raw,
    run,
    dense,
    xs,
    ys,
    bacc,
    bstage,
    fstage,
    bland,
    fland,
    zstage,
    zland,
    facc,
    beta_t,
    score,
    table,
    idx,
    table_sem,
    tile_sem,
    send_sem,
    recv_sem,
):
    slots, blk, _ = raw.shape
    n_row = ys.shape[1]
    chips = n_row // 2
    plane = bstage.shape[1]
    side = round(plane**0.5)
    n_col = 2 * plane
    parts = tile_sem.shape[0]
    chunk = slots // parts
    steps = far_first(side)
    r = lax.axis_index("row")
    c = lax.axis_index("col")
    high, core = r // 2, r % 2
    sibling = (core + 1) % 2
    z = c // plane
    y = (c % plane) // side
    x = c % side
    other = (z + 1) % 2
    yx = y * side + x

    def stepped(i):
        dy, dx = steps[i]
        return ((y + dy) % side) * side + (x + dx) % side

    def chip(k):
        return (high + k) % chips

    def rows_of(k):
        return pl.ds(pl.multiple_of(chip(k) * 2 * blk, 2 * blk), 2 * blk)

    def tile_copy(i):
        part = pl.ds(i * chunk, chunk)
        return pltpu.make_async_copy(tiles.at[part], raw.at[part], tile_sem.at[i])

    for i in range(parts):
        tile_copy(i).start()

    def send(src, dst, t, kind, device):
        pltpu.make_async_remote_copy(
            src_ref=src,
            dst_ref=dst,
            send_sem=send_sem.at[t, kind],
            recv_sem=recv_sem.at[t, kind],
            device_id=device,
            device_id_type=MESH,
        ).start()

    def moved(t, kind):
        if kind in (XOWN, XOTHER, POTHER, POWN):
            return bland.at[t, 0, pl.ds(0, plane - 1)]
        if kind == PZ:
            return zland.at[t]
        count = {XZ: 1, XSIB: 1, XFAR: 2, XNEAR: n_row - 4, PROW: n_row - 1}[kind]
        return fland.at[t, pl.ds(0, count)]

    def arrived(t, kind):
        ref = moved(t, kind)
        pltpu.make_async_copy(ref, ref, recv_sem.at[t, kind]).wait()

    def left(t, kind):
        ref = moved(t, kind)
        pltpu.make_async_copy(ref, ref, send_sem.at[t, kind]).wait()

    barrier = pltpu.get_barrier_semaphore()

    def greet(device):
        pl.semaphore_signal(barrier, inc=1, device_id=device, device_id_type=MESH)

    for off in range(1, n_row):
        greet(((r + off) % n_row, c))
    for i in range(plane - 1):
        greet((r, z * plane + stepped(i)))
    greet((r, other * plane + yx))

    def order_slots():
        n = slots
        along = lax.broadcasted_iota(jnp.int32, (1, n), 1)
        key = jnp.where(along < live[...], block_rows[...] * n_col + block_cols[...], n_row * n_col)
        keys = jnp.broadcast_to(key, (n, n))
        keys_down = keys.T
        across = lax.broadcasted_iota(jnp.int32, (n, n), 1)
        down = lax.broadcasted_iota(jnp.int32, (n, n), 0)
        ahead = (keys_down < keys) | ((keys_down == keys) & (down < across))
        rank = jnp.sum(ahead.astype(jnp.int32), axis=0, keepdims=True)
        hit = jnp.broadcast_to(rank, (n, n)).T == across
        order = jnp.sum(jnp.where(hit, down, 0), axis=0, keepdims=True)
        placed = jnp.sum(jnp.where(hit, keys_down, 0), axis=0, keepdims=True)
        goes_on = (placed == pltpu.roll(placed, 1, axis=1)) & (along > 0)
        upto = jnp.sum((keys_down <= across).astype(jnp.int32), axis=0, keepdims=True)
        there = jnp.sum((keys_down == across).astype(jnp.int32), axis=0, keepdims=True)
        table[0:1, :] = order
        table[1:2, :] = goes_on.astype(jnp.int32)
        table[2:3, :] = jnp.maximum(upto - 1, 0)
        table[3:4, :] = (there > 0).astype(jnp.int32)
        copy = pltpu.make_async_copy(table, idx, table_sem)
        copy.start()
        copy.wait()

    def add_slots():
        for i in range(parts):
            tile_copy(i).wait()

        def add(i, total):
            total = raw[idx[0, i]].astype(F32) + total * idx[1, i].astype(F32)
            run[i] = total.astype(BF16)
            return total

        lax.fori_loop(0, slots, add, jnp.zeros((blk, blk), F32), unroll=4)

    def place():
        @pl.loop(0, n_col)
        def _(cb):
            for rb in range(n_row):
                p = rb * n_col + cb
                dense[cb, rb * blk : (rb + 1) * blk, :] = run[idx[2, p]] * idx[3, p].astype(BF16)

    def spread(t):
        current = score[...].astype(BF16)
        ys[t, r] = current
        xs[t, c] = current
        piece = xs.at[t, c]
        send(piece, piece, t, XZ, (r, other * plane + yx))
        piece = ys.at[t, r]
        send(piece, piece, t, XSIB, (2 * high + sibling, c))
        for k in sorted(range(1, chips), key=lambda k: -min(k, chips - k)):
            kind = XFAR if 2 * k == chips else XNEAR
            for to in range(2):
                send(piece, piece, t, kind, (2 * chip(k) + to, c))
        piece = xs.at[t, c]
        for i in range(plane - 1):
            send(piece, piece, t, XOWN, (r, z * plane + stepped(i)))

    def pass_on(t):
        arrived(t, XZ)
        piece = xs.at[t, other * plane + yx]
        for i in range(plane - 1):
            send(piece, piece, t, XOTHER, (r, z * plane + stepped(i)))

    def pair(zz, g):
        return zz * plane + stepped(2 * g), zz * plane + stepped(2 * g + 1)

    def down(t, ks):
        return jnp.concatenate([ys[t, 2 * chip(k) + i] for k in ks for i in range(2)], axis=1)

    def block(zz, g, ks):
        one, two = pair(zz, g)
        both = [jnp.concatenate([dense[one, rows_of(k), :], dense[two, rows_of(k), :]], axis=1) for k in ks]
        return jnp.concatenate(both, axis=0)

    def transposed(t, planes, ks, first):
        v = down(t, ks)
        for slot, zz in planes:
            for g in range(plane // 2):
                part = jnp.dot(v, block(zz, g, ks), preferred_element_type=F32)
                bacc[slot, g] = part if first else bacc[slot, g] + part

    def transposed_last(t, slot, zz, ks, kind):
        v = down(t, ks)
        for g in range(plane // 2):
            part = jnp.dot(v, block(zz, g, ks), preferred_element_type=F32)
            part = (bacc[slot, g] + part).astype(BF16)
            bstage[slot, 2 * g] = part[:, :blk]
            bstage[slot, 2 * g + 1] = part[:, blk:]
            for i in (2 * g, 2 * g + 1):
                if slot == 0 and i < plane - 1:
                    send(bstage.at[slot, i], bland.at[t, slot, i], t, kind, (r, z * plane + stepped(i)))

    def ship_own(t, which):
        for i in which:
            send(bstage.at[1, i], bland.at[t, 1, i], t, POWN, (r, z * plane + stepped(i)))

    def forward(t, zz, last):
        for m, k in enumerate(sorted(range(chips), key=lambda k: -min(k, chips - k))):
            total = facc[m] if last else jnp.zeros(facc.shape[1:], F32)
            for p in range(plane // 2):
                at = zz * plane + 2 * p
                a = jnp.concatenate([dense[at, rows_of(k), :], dense[at + 1, rows_of(k), :]], axis=1)
                v = jnp.concatenate([xs[t, at], xs[t, at + 1]], axis=1)
                total = total + lax.dot_general(a, v, LAST, preferred_element_type=F32)
            if not last:
                facc[m] = total
                continue
            total = total.T.astype(BF16)
            fstage[2 * m] = total[:, :blk]
            fstage[2 * m + 1] = total[:, blk:]
            if k:
                for to in range(2):
                    send(fstage.at[2 * m + to], fland.at[t, 2 * m + core], t, PROW, (2 * chip(k) + to, c))
                if m == 0:
                    ship_own(t, range(plane - 1))
            else:
                send(fstage.at[2 * m + sibling], fland.at[t, 2 * m], t, PROW, (2 * high + sibling, c))

    def total_of(land, t, count, total):
        for i in range(count):
            total = total + land[t, i].astype(F32)
        return total

    def begin(t):
        arrived(t, XSIB)
        transposed(t, ((0, other), (1, z)), (0,), True)

    beta_t[...] = jnp.broadcast_to(beta[...], (blk, beta.shape[1])).T
    score[...] = seeds[...]
    pl.semaphore_wait(barrier, (n_row - 1) + (plane - 1) + 1)
    spread(0)
    order_slots()
    add_slots()
    pass_on(0)
    place()
    begin(0)

    @pl.loop(0, TERMS)
    def _(t):
        near = tuple(k for k in range(1, chips) if 2 * k != chips)
        if near:
            arrived(t, XNEAR)
            transposed(t, ((0, other), (1, z)), near, False)
        arrived(t, XFAR)
        transposed_last(t, 0, other, (chips // 2,), POTHER)
        arrived(t, XOWN)
        forward(t, z, False)
        transposed_last(t, 1, z, (chips // 2,), POWN)
        arrived(t, XOTHER)
        forward(t, other, True)
        arrived(t, POTHER)
        crossing = total_of(bland.at[:, 0], t, plane - 1, bstage[0, plane - 1].astype(F32))
        zstage[...] = crossing
        send(zstage, zland.at[t], t, PZ, (r, other * plane + yx))
        arrived(t, POWN)
        total = total_of(bland.at[:, 1], t, plane - 1, bstage[1, plane - 1].astype(F32))
        arrived(t, PROW)
        total = total_of(fland, t, n_row - 1, total + fstage[n_row - 2 + core].astype(F32))
        arrived(t, PZ)
        total = total + zland[t]
        score[...] = beta_t[...] * total + seeds[...]

        @pl.when(t < TERMS - 1)
        def _():
            spread(t + 1)
            begin(t + 1)
            pass_on(t + 1)

        for kind in range(10):
            if kind != XNEAR or near:
                left(t, kind)

    out[...] = score[...]


def shards(n_row, n_col, tiles, block_rows, block_cols, live, seeds, beta):
    tiles = tiles[0, 0]
    slots, blk, _ = tiles.shape
    width = seeds.shape[1]
    plane = n_col // 2
    assert slots == n_row * n_col
    vmem = pl.BlockSpec(memory_space=pltpu.VMEM)
    scores = pl.pallas_call(
        kernel,
        out_shape=jax.ShapeDtypeStruct((width, blk), F32),
        in_specs=[
            vmem,
            vmem,
            vmem,
            pl.BlockSpec(memory_space=pl.ANY),
            vmem,
            vmem,
        ],
        out_specs=vmem,
        scratch_shapes=[
            pltpu.VMEM((slots, blk, blk), BF16),
            pltpu.VMEM((slots, blk, blk), BF16),
            pltpu.VMEM((n_col, n_row * blk, blk), BF16),
            pltpu.VMEM((TERMS, n_col, width, blk), BF16),
            pltpu.VMEM((TERMS, n_row, width, blk), BF16),
            pltpu.VMEM((2, plane // 2, width, 2 * blk), F32),
            pltpu.VMEM((2, plane, width, blk), BF16),
            pltpu.VMEM((n_row, width, blk), BF16),
            pltpu.VMEM((TERMS, 2, plane - 1, width, blk), BF16),
            pltpu.VMEM((TERMS, n_row - 1, width, blk), BF16),
            pltpu.VMEM((width, blk), F32),
            pltpu.VMEM((TERMS, width, blk), F32),
            pltpu.VMEM((n_row // 2, 2 * blk, width), F32),
            pltpu.VMEM((width, blk), F32),
            pltpu.VMEM((width, blk), F32),
            pltpu.VMEM((8, slots), jnp.int32),
            pltpu.SMEM((8, slots), jnp.int32),
            pltpu.SemaphoreType.DMA,
            pltpu.SemaphoreType.DMA((4,)),
            pltpu.SemaphoreType.DMA((TERMS, 10)),
            pltpu.SemaphoreType.DMA((TERMS, 10)),
        ],
        compiler_params=pltpu.CompilerParams(
            collective_id=0, has_side_effects=True, vmem_limit_bytes=56 << 20
        ),
        cost_estimate=pl.CostEstimate(
            flops=TERMS * 4 * n_row * n_col * blk * blk * width,
            bytes_accessed=2 * slots * blk * blk,
            transcendentals=0,
        ),
    )(live, block_rows[0], block_cols[0], tiles, seeds.T, beta[None, :])
    return scores.T


def solution(mesh):
    n_row, n_col = mesh.shape["row"], mesh.shape["col"]
    placed = (
        P("row", "col", None, None, None),
        P("row", "col", None),
        P("row", "col", None),
        P("row", "col"),
        P(("col", "row"), None),
        P(),
    )
    return jax.shard_map(
        functools.partial(shards, n_row, n_col),
        mesh=mesh,
        in_specs=placed,
        out_specs=P(("col", "row"), None),
        check_vma=False,
    )
```
